128 devices in a mesh: row: 16 (over y, x), col: 2 (over core), depth: 4 (over z).
Axes of the slice: x: 4, y: 4, z: 4, core: 2. Of those that a mesh axis runs over, the one named last changes fastest.
Arguments:
- amplitudes: float32 [3584, 14336], P('row', ('col', 'depth')), may hold values from -6 to 6
- intermediate: float32 [14336, 14336], P(('col', 'depth'), 'row'), may hold values from -0.046875 to 0.046875
Outputs:
- sigma_cycle: float32 [3584, 14336], P(('col', 'depth'), 'row')
The draws below stay inside these ranges and needn't reach their ends.
All inputs are finite; a program needn't handle non-finite values.
Results may differ from the reference program's by a relative error of at most 0.00011.
Values sent between devices are 32-bit elements; how exact they have to be, the bound alone decides.
A program may use at most 128 MiB of HBM per device.

```python
import jax
import jax.numpy as jnp
from jax import lax

ROWS = 3584
PAIRS = 14336


def with_spikes(result, rng, source, target, blocks, factor):
    owner, partner = [(jnp.arange(result.shape[position]) // (result.shape[position] // blocks)).reshape([-1 if axis == position else 1 for axis in range(result.ndim)]) for position in (source, target)]
    chosen = jax.random.permutation(rng, blocks)[partner]
    strong = (owner == chosen) | (owner == (partner + blocks // 2) % blocks)
    return jnp.where(strong, factor * result, result)


def levels(key, extent, pieces, low, largest):
    gain, own = 1.0, jax.random.fold_in(key, 6)
    for dim, parts in pieces:
        draws = jnp.exp(jax.random.uniform(jax.random.fold_in(own, dim), (parts,), jnp.float32, low / len(pieces), largest / len(pieces)))
        gain = gain * jnp.repeat(draws, extent[dim] // parts).reshape([-1 if axis == dim else 1 for axis in range(len(extent))])
    return gain


def bell_draw(rng, dims, deviation, limit, cuts=(), dtype=jnp.bfloat16):
    loudness = levels(rng, dims, cuts, -0.22, 0.18) if cuts else 1.0
    drawn = jax.random.normal(rng, dims, jnp.float32) * deviation * loudness
    return jnp.minimum(jnp.maximum(drawn, -limit), limit).astype(dtype)


def heavy_noise(rng, dims, scale, reach, pieces, heavy, held_as=jnp.bfloat16):
    result = scale * jax.random.normal(rng, dims, jnp.float32)
    if pieces:
        result = result * levels(rng, dims, pieces, -0.22, 0.18)
    return jnp.clip(with_spikes(result, jax.random.fold_in(rng, 3), *heavy), -reach, reach).astype(held_as)


def setup_inputs(seed: int = 0) -> dict:
    seeds = jax.random.split(jax.random.key(seed), 3)
    return {
        "amplitudes": heavy_noise(seeds[0], (ROWS, PAIRS), 1.0, 6.0, ((0, 16), (1, 8)), (1, 0, 16, 2.0), jnp.float32),
        "intermediate": bell_draw(seeds[1], (PAIRS, PAIRS), PAIRS ** -0.5, 0.046875, ((0, 8), (1, 16)), jnp.float32),
    }


def reference(amplitudes, intermediate):
    cycle_product = jnp.dot(amplitudes, intermediate, preferred_element_type=jnp.float32, precision=lax.Precision.HIGHEST)
    return cycle_product
```

```python
import functools

import jax
import jax.numpy as jnp
from jax import lax
from jax.experimental import pallas as pl
from jax.experimental.pallas import tpu as pltpu
from jax.sharding import PartitionSpec as P

MESH = pl.DeviceIdType.MESH

D1 = (0, 1, 3, 0, 2, 1, 3, 2, 0, 1, 3, 2, 2, 0, 1, 3)
D2 = (0, 0, 0, 1, 0, 1, 1, 1, 3, 3, 3, 3, 2, 2, 2, 2)
PARENT = (0, 0, 0, 0, 1, 1, 2, 4, 0, 1, 2, 4, 7, 3, 5, 6)
STEP1 = (0, 1, -1, 0, 1, 0, 0, 0, 0, 0, 0, 0, 0, 0, 0, 0)
STEP2 = (0, 0, 0, 1, 0, 1, 1, 1, -1, -1, -1, -1, 1, 1, 1, 1)
WAVES = 16
AHEAD = 3
PIECES = 4


def look_up(table, w):
    if isinstance(w, int):
        return table[w]
    value = jnp.int32(table[0])
    for k in range(1, len(table)):
        if table[k] != table[0]:
            value = jnp.where(w == k, jnp.int32(table[k]), value)
    return value


def kernel(a_ref, b_ref, out_ref, g, p, s, r, f, a_hi, a_lo, b_hi, b_lo,
           in_sem, g_send, g_recv, s_send, s_recv, z_send, r_recv, f_recv, out_sem):
    row, core, z = lax.axis_index("row"), lax.axis_index("col"), lax.axis_index("depth")
    y, x = row // 4, row % 4
    piece_rows = a_ref.shape[1]
    depth, columns = b_ref.shape
    block_rows = PIECES * piece_rows

    own = [pltpu.make_async_copy(a_ref.at[q], g.at[0, q], in_sem.at[q]) for q in range(PIECES)]
    for copy in own:
        copy.start()
    stage_waves = depth // block_rows
    b_copies = [
        pltpu.make_async_copy(
            b_ref.at[pl.ds((4 * k + q) * piece_rows, piece_rows)], p.at[WAVES - stage_waves + k, q], in_sem.at[PIECES + 4 * k + q]
        )
        for k in range(stage_waves)
        for q in range(PIECES)
    ]
    for copy in b_copies:
        copy.start()

    def at_row(yy, xx):
        return {"row": ((yy + 8) % 4) * 4 + (xx + 8) % 4}

    barrier = pltpu.get_barrier_semaphore()
    neighbours = [at_row(y, x + 1), at_row(y, x - 1), at_row(y + 1, x), at_row(y - 1, x),
                  {"col": 1 - core}, {"depth": (z + 1) % 4}, {"depth": (z + 3) % 4}]
    for device in neighbours:
        pl.semaphore_signal(barrier, inc=1, device_id=device, device_id_type=MESH)
    pl.semaphore_wait(barrier, len(neighbours))

    def sign(q):
        return 1 - 2 * (q % 2)

    def gather_copy(w, q):
        s1, s2 = sign(q) * look_up(STEP1, w), sign(q) * look_up(STEP2, w)
        sx, sy = (s1, s2) if q < 2 else (s2, s1)
        return pltpu.make_async_remote_copy(
            src_ref=g.at[look_up(PARENT, w), q], dst_ref=g.at[w, q], send_sem=g_send.at[w, q], recv_sem=g_recv.at[w, q],
            device_id=at_row(y + sy, x + sx), device_id_type=MESH,
        )

    def origin(w, q):
        d1, d2 = look_up(D1, w), look_up(D2, w)
        dx, dy = (d1, d2) if q < 2 else (d2, d1)
        xs, ys = (x + 8 - sign(q) * dx) % 4, (y + 8 - sign(q) * dy) % 4
        pair = d1 * 2 + d2 % 2 if q < 2 else (d1 % 2) * 4 + d2
        return ys // 2, 2 * (ys % 2) + xs // 2, xs % 2, pair

    def core_copy(w, q, pair):
        return pltpu.make_async_remote_copy(
            src_ref=p.at[w, q], dst_ref=s.at[pair, q], send_sem=s_send.at[pair, q], recv_sem=s_recv.at[pair, q],
            device_id={"col": 1 - core}, device_id_type=MESH,
        )

    def relay_copy(w, q, half):
        return pltpu.make_async_remote_copy(
            src_ref=p.at[w, q], dst_ref=r.at[half, q], send_sem=z_send.at[1, half, q], recv_sem=r_recv.at[half, q],
            device_id={"depth": (z + 4 + sign(q)) % 4}, device_id_type=MESH,
        )

    def final_copy(w, q, half, which):
        step = -sign(q) if which == 0 else sign(q)
        return pltpu.make_async_remote_copy(
            src_ref=p.at[w, q], dst_ref=f.at[which, half, q], send_sem=z_send.at[2 * which, half, q],
            recv_sem=f_recv.at[which, half, q], device_id={"depth": (z + 4 + step) % 4}, device_id_type=MESH,
        )

    def out_copy(w, q, half):
        return pltpu.make_async_copy(p.at[w, q], out_ref.at[half, q], out_sem.at[half, q])

    def relation(dest_z, q):
        return ((dest_z - z + 4) * sign(q) + 16) % 4

    def send_wave(w):
        for q in range(PIECES):
            gather_copy(w, q).start()

    for copy in own:
        copy.wait()
    for w in range(1, AHEAD + 1):
        send_wave(w)

    for copy in b_copies:
        copy.wait()

    @pl.loop(0, stage_waves)
    def _(k):
        b = p[WAVES - stage_waves + k].reshape(block_rows, columns)
        hi = b.astype(jnp.bfloat16)
        b_hi[pl.ds(pl.multiple_of(k * block_rows, 32), block_rows)] = hi
        b_lo[pl.ds(pl.multiple_of(k * block_rows, 32), block_rows)] = (b - hi.astype(jnp.float32)).astype(jnp.bfloat16)

    def multiply(w):
        for k0 in range(0, depth, 256):
            a = g[w, :, :, k0:k0 + 256].reshape(block_rows, 256)
            hi = a.astype(jnp.bfloat16)
            a_hi[:, k0:k0 + 256] = hi
            a_lo[:, k0:k0 + 256] = (a - hi.astype(jnp.float32)).astype(jnp.bfloat16)
        dot = functools.partial(jnp.dot, preferred_element_type=jnp.float32)
        for n0 in range(0, columns, 256):
            n1 = min(n0 + 256, columns)
            total = dot(a_hi[...], b_hi[:, n0:n1]) + (dot(a_hi[...], b_lo[:, n0:n1]) + dot(a_lo[...], b_hi[:, n0:n1]))
            p[w, :, :, n0:n1] = total.reshape(PIECES, piece_rows, n1 - n0)

    def stage_core(w):
        for q in range(PIECES):
            dest_core, dest_z, half, pair = origin(w, q)
            kind = relation(dest_z, q)

            @pl.when(dest_core == core)
            def _():
                core_copy(w, q, pair).wait_recv()
                p[w, q] = p[w, q] + s[pair, q]

                @pl.when(kind == 2)
                def _():
                    relay_copy(w, q, half).start()

                @pl.when(kind == 3)
                def _():
                    final_copy(w, q, half, 0).start()

    def stage_relay(w):
        for q in range(PIECES):
            dest_core, dest_z, half, _ = origin(w, q)

            @pl.when((dest_core == core) & (relation(dest_z, q) == 1))
            def _():
                relay_copy(w, q, half).wait_recv()
                p[w, q] = p[w, q] + r[half, q]
                final_copy(w, q, half, 1).start()

    def stage_final(w):
        for q in range(PIECES):
            dest_core, dest_z, half, _ = origin(w, q)

            @pl.when((dest_core == core) & (relation(dest_z, q) == 0))
            def _():
                final_copy(w, q, half, 0).wait_recv()
                final_copy(w, q, half, 1).wait_recv()
                p[w, q] = p[w, q] + (f[0, half, q] + f[1, half, q])
                out_copy(w, q, half).start()

    @pl.loop(0, WAVES + 3)
    def _(w):
        @pl.when((w >= 1) & (w <= WAVES))
        def _():
            stage_core(w - 1)

        @pl.when((w >= 2) & (w <= WAVES + 1))
        def _():
            stage_relay(w - 2)

        @pl.when(w >= 3)
        def _():
            stage_final(w - 3)

        @pl.when(w < WAVES)
        def _():
            @pl.when(w >= 1)
            def _():
                for q in range(PIECES):
                    gather_copy(w, q).wait_recv()

                @pl.when(w + AHEAD < WAVES)
                def _():
                    send_wave(w + AHEAD)

            multiply(w)
            for q in range(PIECES):
                dest_core, _, _, pair = origin(w, q)

                @pl.when(dest_core != core)
                def _():
                    core_copy(w, q, pair).start()

    @pl.loop(1, WAVES)
    def _(w):
        for q in range(PIECES):
            gather_copy(w, q).wait_send()

    @pl.loop(0, 8)
    def _(pair):
        for q in range(PIECES):
            core_copy(0, q, pair).wait_send()

    for half in range(2):
        for q in range(PIECES):
            relay_copy(0, q, half).wait_send()
            final_copy(0, q, half, 0).wait_send()
            final_copy(0, q, half, 1).wait_send()
            out_copy(0, q, half).wait()


def per_device(amplitudes, intermediate):
    block_rows, depth = amplitudes.shape
    columns = intermediate.shape[1]
    rows = block_rows // PIECES
    f32, bf16 = jnp.float32, jnp.bfloat16
    dma = pltpu.SemaphoreType.DMA
    result = pl.pallas_call(
        kernel,
        out_shape=jax.ShapeDtypeStruct((2, PIECES, rows, columns), f32),
        in_specs=[pl.BlockSpec(memory_space=pl.ANY)] * 2,
        out_specs=pl.BlockSpec(memory_space=pl.ANY),
        scratch_shapes=[
            pltpu.VMEM((WAVES, PIECES, rows, depth), f32),
            pltpu.VMEM((WAVES, PIECES, rows, columns), f32),
            pltpu.VMEM((WAVES // 2, PIECES, rows, columns), f32),
            pltpu.VMEM((2, PIECES, rows, columns), f32),
            pltpu.VMEM((2, 2, PIECES, rows, columns), f32),
            pltpu.VMEM((block_rows, depth), bf16),
            pltpu.VMEM((block_rows, depth), bf16),
            pltpu.VMEM((depth, columns), bf16),
            pltpu.VMEM((depth, columns), bf16),
            dma((PIECES + 32,)),
            dma((WAVES, PIECES)),
            dma((WAVES, PIECES)),
            dma((WAVES // 2, PIECES)),
            dma((WAVES // 2, PIECES)),
            dma((3, 2, PIECES)),
            dma((2, PIECES)),
            dma((2, 2, PIECES)),
            dma((2, PIECES)),
        ],
        compiler_params=pltpu.CompilerParams(
            collective_id=0, has_side_effects=True, vmem_limit_bytes=60 * 2**20
        ),
        cost_estimate=pl.CostEstimate(flops=34_500_000_000, bytes_accessed=10_000_000, transcendentals=0),
    )(amplitudes.reshape(PIECES, rows, depth), intermediate)
    return result.reshape(2 * block_rows, columns)


def solution(mesh):
    return jax.shard_map(
        per_device,
        mesh=mesh,
        in_specs=(P("row", ("col", "depth")), P(("col", "depth"), "row")),
        out_specs=P(("col", "depth"), "row"),
        check_vma=False,
    )
```

```python
import functools

import jax
import jax.numpy as jnp
from jax import lax
from jax.experimental import pallas as pl
from jax.experimental.pallas import tpu as pltpu
from jax.sharding import PartitionSpec as P

MESH = pl.DeviceIdType.MESH

D1 = (
    (0, 1, 3, 0, 2, 1, 3, 2, 0, 1, 3, 2, 2, 0, 1, 3),
    (0, 1, 3, 0, 2, 1, 3, 2, 0, 1, 3, 2, 2, 0, 1, 3),
    (0, 1, 3, 0, 2, 1, 3, 2, 0, 1, 3, 2, 2, 0, 1, 3),
    (0, 1, 3, 0, 2, 1, 3, 2, 0, 1, 3, 2, 2, 0, 1, 3),
)
D2 = (
    (0, 0, 0, 1, 0, 1, 1, 1, 3, 3, 3, 3, 2, 2, 2, 2),
    (0, 0, 0, 1, 0, 1, 1, 1, 3, 3, 3, 3, 2, 2, 2, 2),
    (0, 0, 0, 1, 0, 1, 1, 1, 3, 3, 3, 3, 2, 2, 2, 2),
    (0, 0, 0, 1, 0, 1, 1, 1, 3, 3, 3, 3, 2, 2, 2, 2),
)
PARENT = (
    (0, 0, 0, 0, 1, 1, 2, 4, 0, 1, 2, 4, 7, 3, 5, 6),
    (0, 0, 0, 0, 1, 1, 2, 4, 0, 1, 2, 4, 7, 3, 5, 6),
    (0, 0, 0, 0, 1, 1, 2, 4, 0, 1, 2, 4, 7, 3, 5, 6),
    (0, 0, 0, 0, 1, 1, 2, 4, 0, 1, 2, 4, 7, 3, 5, 6),
)
STEP1 = (
    (0, 1, -1, 0, 1, 0, 0, 0, 0, 0, 0, 0, 0, 0, 0, 0),
    (0, 1, -1, 0, 1, 0, 0, 0, 0, 0, 0, 0, 0, 0, 0, 0),
    (0, 1, -1, 0, 1, 0, 0, 0, 0, 0, 0, 0, 0, 0, 0, 0),
    (0, 1, -1, 0, 1, 0, 0, 0, 0, 0, 0, 0, 0, 0, 0, 0),
)
STEP2 = (
    (0, 0, 0, 1, 0, 1, 1, 1, -1, -1, -1, -1, 1, 1, 1, 1),
    (0, 0, 0, 1, 0, 1, 1, 1, -1, -1, -1, -1, 1, 1, 1, 1),
    (0, 0, 0, 1, 0, 1, 1, 1, -1, -1, -1, -1, 1, 1, 1, 1),
    (0, 0, 0, 1, 0, 1, 1, 1, -1, -1, -1, -1, 1, 1, 1, 1),
)
WAVES = 16
AHEAD = 3
PIECES = 4


def pack(values, width):
    per = 30 // width
    return [sum(v * 2 ** (width * k) for k, v in enumerate(values[i:i + per])) for i in range(0, len(values), per)]


def unpack(words, w, width):
    per = 30 // width
    if isinstance(w, int):
        word, w = words[w // per], w % per
    else:
        word, base = jnp.int32(words[0]), jnp.int32(0)
        for k in range(1, len(words)):
            word = jnp.where(w >= k * per, jnp.int32(words[k]), word)
            base = jnp.where(w >= k * per, jnp.int32(k * per), base)
        w = w - base
    return (jnp.int32(word) >> (width * w)) & (2 ** width - 1)


def kernel(a_ref, b_ref, out_ref, g, p, s, r, f, a_hi, a_lo, b_hi, b_lo,
           in_sem, g_send, g_recv, s_send, s_recv, z_send, r_recv, f_recv):
    row, core, z = lax.axis_index("row"), lax.axis_index("col"), lax.axis_index("depth")
    y, x = row // 4, row % 4
    piece_rows = a_ref.shape[1]
    depth, columns = b_ref.shape
    block_rows = PIECES * piece_rows

    own = [pltpu.make_async_copy(a_ref.at[q], g.at[0, q], in_sem.at[q]) for q in range(PIECES)]
    for copy in own:
        copy.start()
    stage_waves = depth // block_rows
    b_copies = [
        pltpu.make_async_copy(
            b_ref.at[pl.ds((4 * k + q) * piece_rows, piece_rows)], p.at[WAVES - stage_waves + k, q], in_sem.at[PIECES + 4 * k + q]
        )
        for k in range(stage_waves)
        for q in range(PIECES)
    ]
    for copy in b_copies:
        copy.start()

    def at_row(yy, xx):
        return {"row": ((yy + 8) % 4) * 4 + (xx + 8) % 4}

    barrier = pltpu.get_barrier_semaphore()
    neighbours = [at_row(y, x + 1), at_row(y, x - 1), at_row(y + 1, x), at_row(y - 1, x),
                  {"col": 1 - core}, {"depth": (z + 1) % 4}, {"depth": (z + 3) % 4}]
    for device in neighbours:
        pl.semaphore_signal(barrier, inc=1, device_id=device, device_id_type=MESH)
    pl.semaphore_wait(barrier, len(neighbours))

    def sign(q):
        return 1 - 2 * (q % 2)

    plane = [(y * 4 + ((x + 1) & 3)), (y * 4 + ((x + 3) & 3)), (((y + 1) & 3) * 4 + x), (((y + 3) & 3) * 4 + x)]
    words = pack(plane, 4)

    def link(q, w):
        s1, s2 = sign(q) * STEP1[q][w], sign(q) * STEP2[q][w]
        sx, sy = (s1, s2) if q < 2 else (s2, s1)
        return 0 if sx == 1 else 1 if sx == -1 else 2 if sy == 1 else 3

    links = [pack([link(q, w) for w in range(WAVES)], 2) for q in range(PIECES)]
    parents = [pack(PARENT[q], 4) for q in range(PIECES)]

    def gather_copy(w, q, own=False):
        return pltpu.make_async_remote_copy(
            src_ref=a_ref.at[q] if own else g.at[unpack(parents[q], w, 4), q], dst_ref=g.at[w, q],
            send_sem=g_send.at[w, q], recv_sem=g_recv.at[w, q],
            device_id={"row": unpack(words, unpack(links[q], w, 2), 4)}, device_id_type=MESH,
        )

    codes, pairs = [], []
    for q in range(PIECES):
        values = []
        for w in range(WAVES):
            dx, dy = (D1[q][w], D2[q][w]) if q < 2 else (D2[q][w], D1[q][w])
            xs, ys = (x + 4 - sign(q) * dx) & 3, (y + 4 - sign(q) * dy) & 3
            keep = 1 - (((ys >> 1) + core) & 1)
            kind = ((2 * (ys & 1) + (xs >> 1) - z + 4) * sign(q) + 16) & 3
            values.append(keep + 2 * kind + 8 * (xs & 1))
        codes.append(pack(values, 4))
        pairs.append(pack([D1[q][w] * 2 + D2[q][w] % 2 if q < 2 else (D1[q][w] % 2) * 4 + D2[q][w] for w in range(WAVES)], 3))

    def origin(w, q):
        code = unpack(codes[q], w, 4)
        return code & 7, code >> 3, unpack(pairs[q], w, 3)

    def core_copy(w, q, pair):
        return pltpu.make_async_remote_copy(
            src_ref=p.at[w, q], dst_ref=s.at[pair, q], send_sem=s_send.at[pair, q], recv_sem=s_recv.at[pair, q],
            device_id={"col": 1 - core}, device_id_type=MESH,
        )

    def relay_copy(w, q, half):
        return pltpu.make_async_remote_copy(
            src_ref=p.at[w, q], dst_ref=r.at[half, q], send_sem=z_send.at[1, half, q], recv_sem=r_recv.at[half, q],
            device_id={"depth": (z + 4 + sign(q)) % 4}, device_id_type=MESH,
        )

    def final_copy(w, q, half, which):
        step = -sign(q) if which == 0 else sign(q)
        return pltpu.make_async_remote_copy(
            src_ref=p.at[w, q], dst_ref=f.at[which, half, q], send_sem=z_send.at[2 * which, half, q],
            recv_sem=f_recv.at[which, half, q], device_id={"depth": (z + 4 + step) % 4}, device_id_type=MESH,
        )

    def send_wave(w):
        for q in range(PIECES):
            gather_copy(w, q).start()

    for w in range(1, AHEAD + 1):
        for q in range(PIECES):
            gather_copy(w, q, own=True).start()

    for copy in b_copies:
        copy.wait()

    @pl.loop(0, stage_waves)
    def _(k):
        b = p[WAVES - stage_waves + k].reshape(block_rows, columns)
        hi = b.astype(jnp.bfloat16)
        b_hi[pl.ds(pl.multiple_of(k * block_rows, 32), block_rows)] = hi
        b_lo[pl.ds(pl.multiple_of(k * block_rows, 32), block_rows)] = (b - hi.astype(jnp.float32)).astype(jnp.bfloat16)

    for copy in own:
        copy.wait()

    def multiply(w):
        for k0 in range(0, depth, 256):
            a = g[w, :, :, k0:k0 + 256].reshape(block_rows, 256)
            hi = a.astype(jnp.bfloat16)
            a_hi[:, k0:k0 + 256] = hi
            a_lo[:, k0:k0 + 256] = (a - hi.astype(jnp.float32)).astype(jnp.bfloat16)
        dot = functools.partial(jnp.dot, preferred_element_type=jnp.float32)
        for n0 in range(0, columns, 256):
            n1 = min(n0 + 256, columns)
            total = dot(a_hi[...], b_hi[:, n0:n1]) + (dot(a_hi[...], b_lo[:, n0:n1]) + dot(a_lo[...], b_hi[:, n0:n1]))
            p[w, :, :, n0:n1] = total.reshape(PIECES, piece_rows, n1 - n0)

    def stage_core(w):
        for q in range(PIECES):
            code, half, pair = origin(w, q)

            @pl.when((code & 1) == 1)
            def _():
                core_copy(w, q, pair).wait_recv()
                p[w, q] = p[w, q] + s[pair, q]

                @pl.when(code == 5)
                def _():
                    relay_copy(w, q, half).start()

                @pl.when(code == 7)
                def _():
                    final_copy(w, q, half, 0).start()

    def stage_relay(w):
        for q in range(PIECES):
            code, half, _ = origin(w, q)

            @pl.when(code == 3)
            def _():
                relay_copy(w, q, half).wait_recv()
                p[w, q] = p[w, q] + r[half, q]
                final_copy(w, q, half, 1).start()

    def stage_final(w):
        for q in range(PIECES):
            code, half, _ = origin(w, q)

            @pl.when(code == 1)
            def _():
                final_copy(w, q, half, 0).wait_recv()
                final_copy(w, q, half, 1).wait_recv()
                out_ref[half, q] = p[w, q] + (f[0, half, q] + f[1, half, q])

    @pl.loop(0, WAVES + 3)
    def _(w):
        @pl.when((w >= 1) & (w <= WAVES))
        def _():
            stage_core(w - 1)

        @pl.when((w >= 2) & (w <= WAVES + 1))
        def _():
            stage_relay(w - 2)

        @pl.when(w >= 3)
        def _():
            stage_final(w - 3)

        @pl.when(w < WAVES)
        def _():
            @pl.when(w >= 1)
            def _():
                for q in range(PIECES):
                    gather_copy(w, q).wait_recv()

                @pl.when(w + AHEAD < WAVES)
                def _():
                    send_wave(w + AHEAD)

            multiply(w)
            for q in range(PIECES):
                code, _, pair = origin(w, q)

                @pl.when((code & 1) == 0)
                def _():
                    core_copy(w, q, pair).start()

    @pl.loop(1, WAVES)
    def _(w):
        for q in range(PIECES):
            gather_copy(w, q).wait_send()

    @pl.loop(0, 8)
    def _(pair):
        for q in range(PIECES):
            core_copy(0, q, pair).wait_send()

    for half in range(2):
        for q in range(PIECES):
            relay_copy(0, q, half).wait_send()
            final_copy(0, q, half, 0).wait_send()
            final_copy(0, q, half, 1).wait_send()


def per_device(amplitudes, intermediate):
    block_rows, depth = amplitudes.shape
    columns = intermediate.shape[1]
    rows = block_rows // PIECES
    f32, bf16 = jnp.float32, jnp.bfloat16
    dma = pltpu.SemaphoreType.DMA
    result = pl.pallas_call(
        kernel,
        out_shape=pltpu.VMEM((2, PIECES, rows, columns), f32),
        in_specs=[pl.BlockSpec(memory_space=pl.ANY)] * 2,
        out_specs=pl.BlockSpec(memory_space=pltpu.VMEM),
        scratch_shapes=[
            pltpu.VMEM((WAVES, PIECES, rows, depth), f32),
            pltpu.VMEM((WAVES, PIECES, rows, columns), f32),
            pltpu.VMEM((WAVES // 2, PIECES, rows, columns), f32),
            pltpu.VMEM((2, PIECES, rows, columns), f32),
            pltpu.VMEM((2, 2, PIECES, rows, columns), f32),
            pltpu.VMEM((block_rows, depth), bf16),
            pltpu.VMEM((block_rows, depth), bf16),
            pltpu.VMEM((depth, columns), bf16),
            pltpu.VMEM((depth, columns), bf16),
            dma((PIECES + 32,)),
            dma((WAVES, PIECES)),
            dma((WAVES, PIECES)),
            dma((WAVES // 2, PIECES)),
            dma((WAVES // 2, PIECES)),
            dma((3, 2, PIECES)),
            dma((2, PIECES)),
            dma((2, 2, PIECES)),
        ],
        compiler_params=pltpu.CompilerParams(
            collective_id=0, has_side_effects=True, vmem_limit_bytes=60 * 2**20
        ),
        cost_estimate=pl.CostEstimate(flops=34_500_000_000, bytes_accessed=10_000_000, transcendentals=0),
    )(amplitudes.reshape(PIECES, rows, depth), intermediate)
    return result.reshape(2 * block_rows, columns)


def solution(mesh):
    return jax.shard_map(
        per_device,
        mesh=mesh,
        in_specs=(P("row", ("col", "depth")), P(("col", "depth"), "row")),
        out_specs=P(("col", "depth"), "row"),
        check_vma=False,
    )
```

```python
import functools

import jax
import jax.numpy as jnp
from jax import lax
from jax.experimental import pallas as pl
from jax.experimental.pallas import tpu as pltpu
from jax.sharding import PartitionSpec as P

MESH = pl.DeviceIdType.MESH

D1 = (
    (0, 1, 3, 0, 2, 1, 3, 2, 0, 1, 3, 2, 2, 0, 1, 3),
    (0, 1, 3, 0, 2, 1, 3, 2, 0, 1, 3, 2, 2, 0, 1, 3),
    (0, 1, 3, 0, 2, 1, 3, 2, 0, 1, 3, 2, 2, 0, 1, 3),
    (0, 1, 3, 0, 2, 1, 3, 2, 0, 1, 3, 2, 2, 0, 1, 3),
)
D2 = (
    (0, 0, 0, 1, 0, 1, 1, 1, 3, 3, 3, 3, 2, 2, 2, 2),
    (0, 0, 0, 1, 0, 1, 1, 1, 3, 3, 3, 3, 2, 2, 2, 2),
    (0, 0, 0, 1, 0, 1, 1, 1, 3, 3, 3, 3, 2, 2, 2, 2),
    (0, 0, 0, 1, 0, 1, 1, 1, 3, 3, 3, 3, 2, 2, 2, 2),
)
PARENT = (
    (0, 0, 0, 0, 1, 1, 2, 4, 0, 1, 2, 4, 7, 3, 5, 6),
    (0, 0, 0, 0, 1, 1, 2, 4, 0, 1, 2, 4, 7, 3, 5, 6),
    (0, 0, 0, 0, 1, 1, 2, 4, 0, 1, 2, 4, 7, 3, 5, 6),
    (0, 0, 0, 0, 1, 1, 2, 4, 0, 1, 2, 4, 7, 3, 5, 6),
)
STEP1 = (
    (0, 1, -1, 0, 1, 0, 0, 0, 0, 0, 0, 0, 0, 0, 0, 0),
    (0, 1, -1, 0, 1, 0, 0, 0, 0, 0, 0, 0, 0, 0, 0, 0),
    (0, 1, -1, 0, 1, 0, 0, 0, 0, 0, 0, 0, 0, 0, 0, 0),
    (0, 1, -1, 0, 1, 0, 0, 0, 0, 0, 0, 0, 0, 0, 0, 0),
)
STEP2 = (
    (0, 0, 0, 1, 0, 1, 1, 1, -1, -1, -1, -1, 1, 1, 1, 1),
    (0, 0, 0, 1, 0, 1, 1, 1, -1, -1, -1, -1, 1, 1, 1, 1),
    (0, 0, 0, 1, 0, 1, 1, 1, -1, -1, -1, -1, 1, 1, 1, 1),
    (0, 0, 0, 1, 0, 1, 1, 1, -1, -1, -1, -1, 1, 1, 1, 1),
)
WAVES = 16
AHEAD = 3
PIECES = 4


def pack(values, width):
    per = 30 // width
    return [sum(v * 2 ** (width * k) for k, v in enumerate(values[i:i + per])) for i in range(0, len(values), per)]


def unpack(words, w, width):
    per = 30 // width
    if isinstance(w, int):
        word, w = words[w // per], w % per
    else:
        word, base = jnp.int32(words[0]), jnp.int32(0)
        for k in range(1, len(words)):
            word = jnp.where(w >= k * per, jnp.int32(words[k]), word)
            base = jnp.where(w >= k * per, jnp.int32(k * per), base)
        w = w - base
    return (jnp.int32(word) >> (width * w)) & (2 ** width - 1)


def kernel(a_ref, b_ref, out_ref, g, p, s, r, f, a_hi, a_lo, b_hi, b_lo,
           in_sem, g_send, g_recv, s_send, s_recv, z_send, r_recv, f_recv):
    row, core, z = lax.axis_index("row"), lax.axis_index("col"), lax.axis_index("depth")
    y, x = row >> 2, row & 3
    piece_rows = a_ref.shape[1]
    depth, columns = b_ref.shape
    block_rows = PIECES * piece_rows

    def at_row(yy, xx):
        return {"row": ((yy + 4) & 3) * 4 + ((xx + 4) & 3)}

    barrier = pltpu.get_barrier_semaphore()
    neighbours = [at_row(y, x + 1), at_row(y, x - 1), at_row(y + 1, x), at_row(y - 1, x),
                  {"col": 1 - core}, {"depth": (z + 1) % 4}, {"depth": (z + 3) % 4}]
    for device in neighbours:
        pl.semaphore_signal(barrier, inc=1, device_id=device, device_id_type=MESH)
    pl.semaphore_wait(barrier, len(neighbours))

    def sign(q):
        return 1 - 2 * (q % 2)

    plane = [(y * 4 + ((x + 1) & 3)), (y * 4 + ((x + 3) & 3)), (((y + 1) & 3) * 4 + x), (((y + 3) & 3) * 4 + x)]
    words = pack(plane, 4)

    def link(q, w):
        s1, s2 = sign(q) * STEP1[q][w], sign(q) * STEP2[q][w]
        sx, sy = (s1, s2) if q < 2 else (s2, s1)
        return 0 if sx == 1 else 1 if sx == -1 else 2 if sy == 1 else 3

    links = [pack([link(q, w) for w in range(WAVES)], 2) for q in range(PIECES)]
    parents = [pack(PARENT[q], 4) for q in range(PIECES)]

    def gather_copy(w, q, own=False):
        return pltpu.make_async_remote_copy(
            src_ref=a_ref.at[q] if own else g.at[unpack(parents[q], w, 4), q], dst_ref=g.at[w, q],
            send_sem=g_send.at[w, q], recv_sem=g_recv.at[w, q],
            device_id={"row": unpack(words, unpack(links[q], w, 2), 4)}, device_id_type=MESH,
        )

    def origin(w, q):
        code = unpack(codes[q], w, 4)
        return code & 7, code >> 3, unpack(pairs[q], w, 3)

    def core_copy(w, q, pair):
        return pltpu.make_async_remote_copy(
            src_ref=p.at[w, q], dst_ref=s.at[pair, q], send_sem=s_send.at[pair, q], recv_sem=s_recv.at[pair, q],
            device_id={"col": 1 - core}, device_id_type=MESH,
        )

    cut = (columns // 256 + 1) // 2 * 256
    parts = (pl.ds(0, cut), pl.ds(cut, columns - cut))

    def relay_copy(w, q, half, i):
        return pltpu.make_async_remote_copy(
            src_ref=p.at[w, q, :, parts[i]], dst_ref=r.at[half, q, :, parts[i]], send_sem=z_send.at[i, 1, half, q],
            recv_sem=r_recv.at[i, half, q], device_id={"depth": (z + 4 + sign(q)) & 3}, device_id_type=MESH,
        )

    def final_copy(w, q, half, which, i):
        step = -sign(q) if which == 0 else sign(q)
        return pltpu.make_async_remote_copy(
            src_ref=p.at[w, q, :, parts[i]], dst_ref=f.at[which, half, q, :, parts[i]], send_sem=z_send.at[i, 2 * which, half, q],
            recv_sem=f_recv.at[i, which, half, q], device_id={"depth": (z + 4 + step) & 3}, device_id_type=MESH,
        )

    def send_wave(w):
        for q in range(PIECES):
            gather_copy(w, q).start()

    for w in range(1, AHEAD + 1):
        for q in range(PIECES):
            gather_copy(w, q, own=True).start()

    own = [pltpu.make_async_copy(a_ref.at[q], g.at[0, q], in_sem.at[q]) for q in range(PIECES)]
    for copy in own:
        copy.start()
    stage_waves = depth // block_rows
    b_copies = [
        pltpu.make_async_copy(
            b_ref.at[pl.ds((4 * k + q) * piece_rows, piece_rows)], p.at[WAVES - stage_waves + k, q], in_sem.at[PIECES + 4 * k + q]
        )
        for k in range(stage_waves)
        for q in range(PIECES)
    ]
    for copy in b_copies:
        copy.start()

    codes, pairs = [], []
    for q in range(PIECES):
        values = []
        for w in range(WAVES):
            dx, dy = (D1[q][w], D2[q][w]) if q < 2 else (D2[q][w], D1[q][w])
            xs, ys = (x + 4 - sign(q) * dx) & 3, (y + 4 - sign(q) * dy) & 3
            keep = 1 - (((ys >> 1) + core) & 1)
            kind = ((2 * (ys & 1) + (xs >> 1) - z + 4) * sign(q) + 16) & 3
            values.append(keep + 2 * kind + 8 * (xs & 1))
        codes.append(pack(values, 4))
        pairs.append(pack([D1[q][w] * 2 + D2[q][w] % 2 if q < 2 else (D1[q][w] % 2) * 4 + D2[q][w] for w in range(WAVES)], 3))

    for copy in b_copies:
        copy.wait()

    @pl.loop(0, stage_waves)
    def _(k):
        b = p[WAVES - stage_waves + k].reshape(block_rows, columns)
        hi = b.astype(jnp.bfloat16)
        b_hi[pl.ds(pl.multiple_of(k * block_rows, 32), block_rows)] = hi
        b_lo[pl.ds(pl.multiple_of(k * block_rows, 32), block_rows)] = (b - hi.astype(jnp.float32)).astype(jnp.bfloat16)

    for copy in own:
        copy.wait()

    def multiply(w):
        for k0 in range(0, depth, 256):
            a = g[w, :, :, k0:k0 + 256].reshape(block_rows, 256)
            hi = a.astype(jnp.bfloat16)
            a_hi[:, k0:k0 + 256] = hi
            a_lo[:, k0:k0 + 256] = (a - hi.astype(jnp.float32)).astype(jnp.bfloat16)
        dot = functools.partial(jnp.dot, preferred_element_type=jnp.float32)
        for n0 in range(0, columns, 512):
            n1 = min(n0 + 512, columns)
            total = dot(a_hi[...], b_hi[:, n0:n1]) + (dot(a_hi[...], b_lo[:, n0:n1]) + dot(a_lo[...], b_hi[:, n0:n1]))
            p[w, :, :, n0:n1] = total.reshape(PIECES, piece_rows, n1 - n0)

    def stage_core(w):
        for q in range(PIECES):
            code, half, pair = origin(w, q)

            @pl.when((code & 1) == 1)
            def _():
                core_copy(w, q, pair).wait_recv()
                p[w, q] = p[w, q] + s[pair, q]

                @pl.when(code == 5)
                def _():
                    for i in range(2):
                        relay_copy(w, q, half, i).start()

                @pl.when(code == 7)
                def _():
                    for i in range(2):
                        final_copy(w, q, half, 0, i).start()

    def stage_relay(w):
        for i in range(2):
            for q in range(PIECES):
                code, half, _ = origin(w, q)

                @pl.when(code == 3)
                def _():
                    relay_copy(w, q, half, i).wait_recv()
                    p[w, q, :, parts[i]] = p[w, q, :, parts[i]] + r[half, q, :, parts[i]]
                    final_copy(w, q, half, 1, i).start()

    def stage_final(w):
        for q in range(PIECES):
            code, half, _ = origin(w, q)

            @pl.when(code == 1)
            def _():
                for i in range(2):
                    for which in range(2):
                        final_copy(w, q, half, which, i).wait_recv()
                out_ref[half, q] = p[w, q] + (f[0, half, q] + f[1, half, q])

    @pl.loop(0, WAVES + 3)
    def _(w):
        @pl.when((w >= 1) & (w <= WAVES))
        def _():
            stage_core(w - 1)

        @pl.when((w >= 2) & (w <= WAVES + 1))
        def _():
            stage_relay(w - 2)

        @pl.when(w >= 3)
        def _():
            stage_final(w - 3)

        @pl.when(w < WAVES)
        def _():
            @pl.when(w >= 1)
            def _():
                for q in range(PIECES):
                    gather_copy(w, q).wait_recv()

                @pl.when(w + AHEAD < WAVES)
                def _():
                    send_wave(w + AHEAD)

            multiply(w)
            for q in range(PIECES):
                code, _, pair = origin(w, q)

                @pl.when((code & 1) == 0)
                def _():
                    core_copy(w, q, pair).start()

    @pl.loop(1, WAVES)
    def _(w):
        for q in range(PIECES):
            gather_copy(w, q).wait_send()

    @pl.loop(0, 8)
    def _(pair):
        for q in range(PIECES):
            core_copy(0, q, pair).wait_send()

    for half in range(2):
        for q in range(PIECES):
            for i in range(2):
                relay_copy(0, q, half, i).wait_send()
                final_copy(0, q, half, 0, i).wait_send()
                final_copy(0, q, half, 1, i).wait_send()


def per_device(amplitudes, intermediate):
    block_rows, depth = amplitudes.shape
    columns = intermediate.shape[1]
    rows = block_rows // PIECES
    f32, bf16 = jnp.float32, jnp.bfloat16
    dma = pltpu.SemaphoreType.DMA
    result = pl.pallas_call(
        kernel,
        out_shape=pltpu.VMEM((2, PIECES, rows, columns), f32),
        in_specs=[pl.BlockSpec(memory_space=pl.ANY)] * 2,
        out_specs=pl.BlockSpec(memory_space=pltpu.VMEM),
        scratch_shapes=[
            pltpu.VMEM((WAVES, PIECES, rows, depth), f32),
            pltpu.VMEM((WAVES, PIECES, rows, columns), f32),
            pltpu.VMEM((WAVES // 2, PIECES, rows, columns), f32),
            pltpu.VMEM((2, PIECES, rows, columns), f32),
            pltpu.VMEM((2, 2, PIECES, rows, columns), f32),
            pltpu.VMEM((block_rows, depth), bf16),
            pltpu.VMEM((block_rows, depth), bf16),
            pltpu.VMEM((depth, columns), bf16),
            pltpu.VMEM((depth, columns), bf16),
            dma((PIECES + 32,)),
            dma((WAVES, PIECES)),
            dma((WAVES, PIECES)),
            dma((WAVES // 2, PIECES)),
            dma((WAVES // 2, PIECES)),
            dma((2, 3, 2, PIECES)),
            dma((2, 2, PIECES)),
            dma((2, 2, 2, PIECES)),
        ],
        compiler_params=pltpu.CompilerParams(
            collective_id=0, has_side_effects=True, vmem_limit_bytes=60 * 2**20
        ),
        cost_estimate=pl.CostEstimate(flops=34_500_000_000, bytes_accessed=10_000_000, transcendentals=0),
    )(amplitudes.reshape(PIECES, rows, depth), intermediate)
    return result.reshape(2 * block_rows, columns)


def solution(mesh):
    return jax.shard_map(
        per_device,
        mesh=mesh,
        in_specs=(P("row", ("col", "depth")), P(("col", "depth"), "row")),
        out_specs=P(("col", "depth"), "row"),
        check_vma=False,
    )
```

```python
import functools

import jax
import jax.numpy as jnp
from jax import lax
from jax.experimental import pallas as pl
from jax.experimental.pallas import tpu as pltpu
from jax.sharding import PartitionSpec as P

MESH = pl.DeviceIdType.MESH

D1 = (
    (0, 1, 3, 0, 2, 1, 3, 2, 0, 1, 3, 2, 2, 0, 1, 3),
    (0, 1, 3, 0, 2, 1, 3, 2, 0, 1, 3, 2, 2, 0, 1, 3),
    (0, 1, 3, 0, 2, 1, 3, 2, 0, 1, 3, 2, 2, 0, 1, 3),
    (0, 1, 3, 0, 2, 1, 3, 2, 0, 1, 3, 2, 2, 0, 1, 3),
)
D2 = (
    (0, 0, 0, 1, 0, 1, 1, 1, 3, 3, 3, 3, 2, 2, 2, 2),
    (0, 0, 0, 1, 0, 1, 1, 1, 3, 3, 3, 3, 2, 2, 2, 2),
    (0, 0, 0, 1, 0, 1, 1, 1, 3, 3, 3, 3, 2, 2, 2, 2),
    (0, 0, 0, 1, 0, 1, 1, 1, 3, 3, 3, 3, 2, 2, 2, 2),
)
PARENT = (
    (0, 0, 0, 0, 1, 1, 2, 4, 0, 1, 2, 4, 7, 3, 5, 6),
    (0, 0, 0, 0, 1, 1, 2, 4, 0, 1, 2, 4, 7, 3, 5, 6),
    (0, 0, 0, 0, 1, 1, 2, 4, 0, 1, 2, 4, 7, 3, 5, 6),
    (0, 0, 0, 0, 1, 1, 2, 4, 0, 1, 2, 4, 7, 3, 5, 6),
)
STEP1 = (
    (0, 1, -1, 0, 1, 0, 0, 0, 0, 0, 0, 0, 0, 0, 0, 0),
    (0, 1, -1, 0, 1, 0, 0, 0, 0, 0, 0, 0, 0, 0, 0, 0),
    (0, 1, -1, 0, 1, 0, 0, 0, 0, 0, 0, 0, 0, 0, 0, 0),
    (0, 1, -1, 0, 1, 0, 0, 0, 0, 0, 0, 0, 0, 0, 0, 0),
)
STEP2 = (
    (0, 0, 0, 1, 0, 1, 1, 1, -1, -1, -1, -1, 1, 1, 1, 1),
    (0, 0, 0, 1, 0, 1, 1, 1, -1, -1, -1, -1, 1, 1, 1, 1),
    (0, 0, 0, 1, 0, 1, 1, 1, -1, -1, -1, -1, 1, 1, 1, 1),
    (0, 0, 0, 1, 0, 1, 1, 1, -1, -1, -1, -1, 1, 1, 1, 1),
)
WAVES = 16
AHEAD = 3
PIECES = 4


def pack(values, width):
    per = 30 // width
    return [sum(v * 2 ** (width * k) for k, v in enumerate(values[i:i + per])) for i in range(0, len(values), per)]


def unpack(words, w, width):
    per = 30 // width
    if isinstance(w, int):
        word, w = words[w // per], w % per
    else:
        word, base = jnp.int32(words[0]), jnp.int32(0)
        for k in range(1, len(words)):
            word = jnp.where(w >= k * per, jnp.int32(words[k]), word)
            base = jnp.where(w >= k * per, jnp.int32(k * per), base)
        w = w - base
    return (jnp.int32(word) >> (width * w)) & (2 ** width - 1)


def kernel(a_ref, b_ref, out_ref, g, p, s, r, f, a_hi, a_lo, b_hi, b_lo,
           in_sem, g_send, g_recv, s_send, s_recv, z_send, r_recv, f_recv):
    row, core, z = lax.axis_index("row"), lax.axis_index("col"), lax.axis_index("depth")
    y, x = row >> 2, row & 3
    piece_rows = a_ref.shape[1]
    depth, columns = b_ref.shape
    block_rows = PIECES * piece_rows

    def at_row(yy, xx):
        return {"row": ((yy + 4) & 3) * 4 + ((xx + 4) & 3)}

    barrier = pltpu.get_barrier_semaphore()
    neighbours = [at_row(y, x + 1), at_row(y, x - 1), at_row(y + 1, x), at_row(y - 1, x),
                  {"col": 1 - core}, {"depth": (z + 1) % 4}, {"depth": (z + 3) % 4}]
    for device in neighbours:
        pl.semaphore_signal(barrier, inc=1, device_id=device, device_id_type=MESH)
    pl.semaphore_wait(barrier, len(neighbours))

    def sign(q):
        return 1 - 2 * (q % 2)

    plane = [(y * 4 + ((x + 1) & 3)), (y * 4 + ((x + 3) & 3)), (((y + 1) & 3) * 4 + x), (((y + 3) & 3) * 4 + x)]
    words = pack(plane, 4)

    def link(q, w):
        s1, s2 = sign(q) * STEP1[q][w], sign(q) * STEP2[q][w]
        sx, sy = (s1, s2) if q < 2 else (s2, s1)
        return 0 if sx == 1 else 1 if sx == -1 else 2 if sy == 1 else 3

    links = [pack([link(q, w) for w in range(WAVES)], 2) for q in range(PIECES)]
    parents = [pack(PARENT[q], 4) for q in range(PIECES)]

    def gather_copy(w, q, own=False):
        return pltpu.make_async_remote_copy(
            src_ref=a_ref.at[q] if own else g.at[unpack(parents[q], w, 4), q], dst_ref=g.at[w, q],
            send_sem=g_send.at[w, q], recv_sem=g_recv.at[w, q],
            device_id={"row": unpack(words, unpack(links[q], w, 2), 4)}, device_id_type=MESH,
        )

    def origin(w, q):
        code = unpack(codes[q], w, 4)
        return code & 7, code >> 3, unpack(pairs[q], w, 3)

    def core_copy(w, q, pair):
        return pltpu.make_async_remote_copy(
            src_ref=p.at[w, q], dst_ref=s.at[pair, q], send_sem=s_send.at[pair, q], recv_sem=s_recv.at[pair, q],
            device_id={"col": 1 - core}, device_id_type=MESH,
        )

    cut = (columns // 256 + 1) // 2 * 256
    parts = (pl.ds(0, cut), pl.ds(cut, columns - cut))

    def relay_copy(w, q, half, i):
        return pltpu.make_async_remote_copy(
            src_ref=p.at[w, q, :, parts[i]], dst_ref=r.at[half, q, :, parts[i]], send_sem=z_send.at[i, 1, half, q],
            recv_sem=r_recv.at[i, half, q], device_id={"depth": (z + 4 + sign(q)) & 3}, device_id_type=MESH,
        )

    def final_copy(w, q, half, which, i):
        step = -sign(q) if which == 0 else sign(q)
        return pltpu.make_async_remote_copy(
            src_ref=p.at[w, q, :, parts[i]], dst_ref=f.at[which, half, q, :, parts[i]], send_sem=z_send.at[i, 2 * which, half, q],
            recv_sem=f_recv.at[i, which, half, q], device_id={"depth": (z + 4 + step) & 3}, device_id_type=MESH,
        )

    def send_wave(w):
        for q in range(PIECES):
            gather_copy(w, q).start()

    for w in range(1, AHEAD + 1):
        for q in range(PIECES):
            gather_copy(w, q, own=True).start()

    own = [pltpu.make_async_copy(a_ref.at[q], g.at[0, q], in_sem.at[q]) for q in range(PIECES)]
    for copy in own:
        copy.start()
    stage_waves = depth // block_rows
    b_copies = [
        pltpu.make_async_copy(
            b_ref.at[pl.ds((4 * k + q) * piece_rows, piece_rows)], p.at[WAVES - stage_waves + k, q], in_sem.at[PIECES + 4 * k + q]
        )
        for k in range(stage_waves)
        for q in range(PIECES)
    ]
    for copy in b_copies:
        copy.start()

    codes, pairs = [], []
    for q in range(PIECES):
        values = []
        for w in range(WAVES):
            dx, dy = (D1[q][w], D2[q][w]) if q < 2 else (D2[q][w], D1[q][w])
            xs, ys = (x + 4 - sign(q) * dx) & 3, (y + 4 - sign(q) * dy) & 3
            keep = 1 - (((ys >> 1) + core) & 1)
            kind = ((2 * (ys & 1) + (xs >> 1) - z + 4) * sign(q) + 16) & 3
            values.append(keep + 2 * kind + 8 * (xs & 1))
        codes.append(pack(values, 4))
        pairs.append(pack([D1[q][w] * 2 + D2[q][w] % 2 if q < 2 else (D1[q][w] % 2) * 4 + D2[q][w] for w in range(WAVES)], 3))

    for copy in b_copies:
        copy.wait()

    @pl.loop(0, stage_waves)
    def _(k):
        b = p[WAVES - stage_waves + k].reshape(block_rows, columns)
        hi = b.astype(jnp.bfloat16)
        b_hi[pl.ds(pl.multiple_of(k * block_rows, 32), block_rows)] = hi
        b_lo[pl.ds(pl.multiple_of(k * block_rows, 32), block_rows)] = (b - hi.astype(jnp.float32)).astype(jnp.bfloat16)

    for copy in own:
        copy.wait()

    def multiply(w):
        for k0 in range(0, depth, 256):
            a = g[w, :, :, k0:k0 + 256].reshape(block_rows, 256)
            hi = a.astype(jnp.bfloat16)
            a_hi[:, k0:k0 + 256] = hi
            a_lo[:, k0:k0 + 256] = (a - hi.astype(jnp.float32)).astype(jnp.bfloat16)
        dot = functools.partial(jnp.dot, preferred_element_type=jnp.float32)
        for n0 in range(0, columns, 256):
            n1 = min(n0 + 256, columns)
            total = dot(a_hi[...], b_hi[:, n0:n1]) + (dot(a_hi[...], b_lo[:, n0:n1]) + dot(a_lo[...], b_hi[:, n0:n1]))
            p[w, :, :, n0:n1] = total.reshape(PIECES, piece_rows, n1 - n0)

    def stage_core(w):
        for i in range(2):
            for q in range(PIECES):
                code, half, pair = origin(w, q)

                @pl.when((code & 1) == 1)
                def _():
                    if i == 0:
                        core_copy(w, q, pair).wait_recv()
                        p[w, q] = p[w, q] + s[pair, q]

                    @pl.when(code == 5)
                    def _():
                        relay_copy(w, q, half, i).start()

                    @pl.when(code == 7)
                    def _():
                        final_copy(w, q, half, 0, i).start()

    def stage_relay(w):
        for i in range(2):
            for q in range(PIECES):
                code, half, _ = origin(w, q)

                @pl.when(code == 3)
                def _():
                    relay_copy(w, q, half, i).wait_recv()
                    p[w, q, :, parts[i]] = p[w, q, :, parts[i]] + r[half, q, :, parts[i]]
                    final_copy(w, q, half, 1, i).start()

    def stage_final(w):
        for q in range(PIECES):
            code, half, _ = origin(w, q)

            @pl.when(code == 1)
            def _():
                for i in range(2):
                    for which in range(2):
                        final_copy(w, q, half, which, i).wait_recv()
                out_ref[half, q] = p[w, q] + (f[0, half, q] + f[1, half, q])

    @pl.loop(0, WAVES + 3)
    def _(w):
        @pl.when((w >= 1) & (w <= WAVES))
        def _():
            stage_core(w - 1)

        @pl.when((w >= 2) & (w <= WAVES + 1))
        def _():
            stage_relay(w - 2)

        @pl.when(w >= 3)
        def _():
            stage_final(w - 3)

        @pl.when(w < WAVES)
        def _():
            @pl.when(w >= 1)
            def _():
                for q in range(PIECES):
                    gather_copy(w, q).wait_recv()

                @pl.when(w + AHEAD < WAVES)
                def _():
                    send_wave(w + AHEAD)

            multiply(w)
            for q in range(PIECES):
                code, _, pair = origin(w, q)

                @pl.when((code & 1) == 0)
                def _():
                    core_copy(w, q, pair).start()

    @pl.loop(1, WAVES)
    def _(w):
        for q in range(PIECES):
            gather_copy(w, q).wait_send()

    @pl.loop(0, 8)
    def _(pair):
        for q in range(PIECES):
            core_copy(0, q, pair).wait_send()

    for half in range(2):
        for q in range(PIECES):
            for i in range(2):
                relay_copy(0, q, half, i).wait_send()
                final_copy(0, q, half, 0, i).wait_send()
                final_copy(0, q, half, 1, i).wait_send()


def per_device(amplitudes, intermediate):
    block_rows, depth = amplitudes.shape
    columns = intermediate.shape[1]
    rows = block_rows // PIECES
    f32, bf16 = jnp.float32, jnp.bfloat16
    dma = pltpu.SemaphoreType.DMA
    result = pl.pallas_call(
        kernel,
        out_shape=pltpu.VMEM((2, PIECES, rows, columns), f32),
        in_specs=[pl.BlockSpec(memory_space=pl.ANY)] * 2,
        out_specs=pl.BlockSpec(memory_space=pltpu.VMEM),
        scratch_shapes=[
            pltpu.VMEM((WAVES, PIECES, rows, depth), f32),
            pltpu.VMEM((WAVES, PIECES, rows, columns), f32),
            pltpu.VMEM((WAVES // 2, PIECES, rows, columns), f32),
            pltpu.VMEM((2, PIECES, rows, columns), f32),
            pltpu.VMEM((2, 2, PIECES, rows, columns), f32),
            pltpu.VMEM((block_rows, depth), bf16),
            pltpu.VMEM((block_rows, depth), bf16),
            pltpu.VMEM((depth, columns), bf16),
            pltpu.VMEM((depth, columns), bf16),
            dma((PIECES + 32,)),
            dma((WAVES, PIECES)),
            dma((WAVES, PIECES)),
            dma((WAVES // 2, PIECES)),
            dma((WAVES // 2, PIECES)),
            dma((2, 3, 2, PIECES)),
            dma((2, 2, PIECES)),
            dma((2, 2, 2, PIECES)),
        ],
        compiler_params=pltpu.CompilerParams(
            collective_id=0, has_side_effects=True, vmem_limit_bytes=60 * 2**20
        ),
        cost_estimate=pl.CostEstimate(flops=34_500_000_000, bytes_accessed=10_000_000, transcendentals=0),
    )(amplitudes.reshape(PIECES, rows, depth), intermediate)
    return result.reshape(2 * block_rows, columns)


def solution(mesh):
    return jax.shard_map(
        per_device,
        mesh=mesh,
        in_specs=(P("row", ("col", "depth")), P(("col", "depth"), "row")),
        out_specs=P(("col", "depth"), "row"),
        check_vma=False,
    )
```
